128 devices in a mesh: ex: 32 (over z, y, x_hi), eig: 4 (over x_lo, core).
Axes of the slice: x: 4 (x_hi: 2, x_lo: 2; x = x_hi * 2 + x_lo), y: 4, z: 4, core: 2. Of those that a mesh axis runs over, the one named last changes fastest.
Arguments:
- layer_inputs: bfloat16 [4096, 14336], P('ex', 'eig'), may hold values from -6 to 6
- out_grads: bfloat16 [4096, 4096], P('eig'), may hold values from -6 to 6
- hidden_basis: bfloat16 [14336, 14336], P('eig', 'ex'), may hold values from -0.046875 to 0.046875
- output_basis: bfloat16 [4096, 4096], P(None, 'ex'), may hold values from -0.09375 to 0.09375
- eigenvalues: float32 [4096, 14336], P(None, 'ex'), may hold values from 1920 to 192000
- query_inputs: bfloat16 [32, 8, 14336], P('ex'), may hold values from -6 to 6
- query_grads: bfloat16 [32, 8, 4096], P('ex'), may hold values from -6 to 6
- query_owner: int32 [4], replicated, may hold values from 0 to 31
- example_lengths: int32 [32, 4], replicated, may hold values from 1 to 64, 128 in all within a row
Outputs:
- token_scores: float32 [4, 4096], P(None, ('eig', 'ex'))
- example_scores: float32 [4, 128], P(None, ('eig', 'ex'))
The draws below stay inside these ranges and needn't reach their ends.
Inputs may be any that keep to these rules, and one draw needn't show every extreme that they name: `example_lengths`: each shard's 4 lengths sum to 128.
All inputs are finite; a program needn't handle non-finite values.
Results may differ from the reference program's by a relative error of at most 0.025.
Values may be sent and summed in bfloat16 or wider, within the bound.
No kernel may reach another device: no remote copies, remote signals or barrier semaphores. Data moves between devices by JAX's collectives and lax.ppermute only.
A program may use at most 192 MiB of HBM per device.

```python
import math
import jax
import jax.numpy as jnp
import numpy as np
from jax import lax

DOUT = 4096
DHID = 14336
TOK_DEV = 128
QTOK = 8
QUERIES = 4
EX_DEV = 4
DAMP = 480
BLOCKS = 4
SLOTS = 32
TOKENS = 4096


def with_ends(array, key, least, top_value):
    dims = array.shape
    index_at = [jax.random.randint(jax.random.fold_in(key, axis), (), 0, dims[axis]) for axis in range(len(dims))]
    array = array.at[tuple(index_at)].set(least)
    longest = dims.index(max(dims))
    index_at[longest] = (index_at[longest] + 1) % dims[longest]
    return array.at[tuple(index_at)].set(top_value)


def block_scale(stream_key, dims, pieces, low, top_value):
    factor_of = 1.0
    for axis_at, parts in pieces:
        draws = jax.random.uniform(jax.random.fold_in(jax.random.fold_in(stream_key, 6), axis_at), (parts,), jnp.float32, low / len(pieces), top_value / len(pieces))
        factor_of = factor_of * jnp.repeat(jnp.exp(draws), dims[axis_at] // parts).reshape((-1,) + (1,) * (len(dims) - 1 - axis_at))
    return factor_of


def split_up(count, total, bound, skew):
    loads = [(1 << 20) // math.isqrt(standing ** skew) + 1 for standing in range(2, count + 1)]
    surplus, counts = total - bound - (count - 1), [1] * (count - 1)
    while surplus > 0:
        free = [i for i in range(count - 1) if counts[i] < bound]
        mass, left = sum([loads[i] for i in free]), surplus
        for i in free:
            addition = min(bound - counts[i], max(1, left * loads[i] // mass), surplus)
            counts[i] = counts[i] + addition
            surplus = surplus - addition
    return np.array([bound] + counts)


def uneven(rng, number_of, total, limit, skew):
    if number_of == 2:
        one = jax.random.randint(rng, (), max(1, total - limit), min(limit, total - 1) + 1)
        return jnp.stack([one, total - one])
    sizes = jnp.asarray(split_up(number_of, total, limit, skew), jnp.int32)
    pairs = (number_of - 1) // 2
    donor, taker = sizes[1:1 + 2 * pairs:2], sizes[2:2 + 2 * pairs:2]
    slack = jnp.minimum(donor - 1, limit - taker)
    moved = jax.random.randint(jax.random.fold_in(rng, 1), (pairs,), 0, 1 << 20) % (slack + 1)
    sizes = sizes.at[1:1 + 2 * pairs:2].set(donor - moved).at[2:2 + 2 * pairs:2].set(taker + moved)
    return sizes[jax.random.permutation(jax.random.fold_in(rng, 2), number_of)]


def gaussian(key, dims, spread, bound, shards=(), held_as=jnp.bfloat16):
    loudness = block_scale(key, dims, shards, -0.22, 0.18) if shards else 1.0
    array = jax.random.normal(key, dims, jnp.float32) * spread * loudness
    return jnp.minimum(jnp.maximum(array, -bound), bound).astype(held_as)


def setup_inputs(seed: int = 0) -> dict:
    seeds = jax.random.split(jax.random.key(seed), 10)
    layer_inputs = gaussian(seeds[0], (TOKENS, DHID), 1.0, 6.0, ((0, 32), (1, 4)))
    out_grads = gaussian(seeds[1], (TOKENS, DOUT), 1.0, 6.0, ((0, 4),))
    hidden_basis = gaussian(seeds[2], (DHID, DHID), DHID ** -0.5, 0.046875, ((0, 4), (1, 32)))
    output_basis = gaussian(seeds[3], (DOUT, DOUT), DOUT ** -0.5, 0.09375, ((1, 32),))
    eigenvalues = jnp.clip(jnp.exp(math.log(192000.0) - 4.6051702 * jax.random.uniform(seeds[4], (DOUT, DHID), jnp.float32) ** block_scale(seeds[4], (DOUT, DHID), ((1, 32),), -0.2, 0.2)), 1920.0, 192000.0)
    query_inputs = gaussian(seeds[5], (SLOTS, QTOK, DHID), 1.0, 6.0, ((0, 32),))
    query_grads = gaussian(seeds[6], (SLOTS, QTOK, DOUT), 1.0, 6.0, ((0, 32),))
    query_owner = with_ends(jax.random.randint(seeds[7], (QUERIES,), 0, SLOTS), jax.random.fold_in(seeds[7], 1), 0, SLOTS - 1).astype(jnp.int32)
    example_lengths = jax.vmap(lambda own: uneven(own, EX_DEV, TOK_DEV, TOK_DEV // 2, 2))(jax.random.split(seeds[8], SLOTS)).reshape((SLOTS, EX_DEV)).astype(jnp.int32)
    return dict(layer_inputs=layer_inputs, out_grads=out_grads, hidden_basis=hidden_basis, output_basis=output_basis, eigenvalues=eigenvalues, query_inputs=query_inputs, query_grads=query_grads, query_owner=query_owner, example_lengths=example_lengths)


def reference(layer_inputs, out_grads, hidden_basis, output_basis, eigenvalues, query_inputs, query_grads, query_owner, example_lengths):
    block_rows = DHID // BLOCKS
    summed = jnp.zeros((TOKENS, DHID), jnp.float32)
    for block_index in range(BLOCKS):
        rows_in = layer_inputs[:, block_index * block_rows:(block_index + 1) * block_rows]
        basis_rows = hidden_basis[block_index * block_rows:(block_index + 1) * block_rows]
        part_sum = jnp.dot(rows_in, basis_rows, preferred_element_type=jnp.float32).astype(jnp.bfloat16)
        part_sum = lax.optimization_barrier(part_sum)
        summed = summed + part_sum.astype(jnp.float32)
    hidden_rot = summed.astype(jnp.bfloat16)
    grad_rot = jnp.dot(out_grads, output_basis, preferred_element_type=jnp.float32).astype(jnp.bfloat16)
    hidden_wide = hidden_rot.astype(jnp.float32)
    token_rows = []
    for query_index in range(QUERIES):
        owner_in = query_inputs[query_owner[query_index]]
        owner_grad = query_grads[query_owner[query_index]]
        outer_sum = jnp.einsum("si,sj->ij", owner_grad.astype(jnp.float32), owner_in.astype(jnp.float32), precision=lax.Precision.HIGHEST)
        precond = (outer_sum / (eigenvalues + DAMP)).astype(jnp.bfloat16)
        mixed_rows = jnp.dot(grad_rot, precond, preferred_element_type=jnp.float32)
        token_rows.append(jnp.sum(mixed_rows * hidden_wide, axis=1))
    token_scores = jnp.stack(token_rows)
    example_ends = jnp.cumsum(example_lengths, axis=1).astype(jnp.int32)
    starts = example_ends - example_lengths
    shard_base = (jnp.arange(SLOTS, dtype=jnp.int32) * TOK_DEV)[:, None]
    token_first = (shard_base + starts).reshape(-1)
    token_last = (shard_base + example_ends).reshape(-1)
    position = jnp.arange(TOKENS, dtype=jnp.int32)
    member = ((position[None, :] >= token_first[:, None]) & (position[None, :] < token_last[:, None])).astype(jnp.float32)
    example_scores = jnp.dot(token_scores, member.T, precision=lax.Precision.HIGHEST)
    return token_scores, example_scores
```

```python
import jax
import jax.numpy as jnp
import numpy as np
from jax import lax
from jax.sharding import Mesh, PartitionSpec as P

DAMP = 480
AXES = ("z", "y", "xh", "xl", "c")
SIZES = (4, 4, 2, 2, 2)


def permutation(move):
    pairs = []
    for source, place in enumerate(np.ndindex(*SIZES)):
        target = move(*place)
        if target is not None:
            target = tuple(a % b for a, b in zip(target, SIZES))
            pairs.append((source, int(np.ravel_multi_index(target, SIZES))))
    return pairs


RING_Z = permutation(lambda z, y, xh, xl, c: (z + 1 - 2 * c, y, xh, xl, c))
RING_Y = permutation(lambda z, y, xh, xl, c: (z, y + 1 - 2 * c, xh, xl, c))
OTHER_XH = permutation(lambda z, y, xh, xl, c: (z, y, xh + 1, xl, c))
OTHER_XL = permutation(lambda z, y, xh, xl, c: (z, y, xh, xl + 1, c))
OTHER_CORE = permutation(lambda z, y, xh, xl, c: (z, y, xh, xl, c + 1))
EIGEN = permutation(
    lambda z, y, xh, xl, c: (z, y, 1 - xh, 1 - xl, c) if c == xh else None
)


def send(value, pairs):
    return lax.ppermute(value, AXES, pairs)


def ring(value, pairs):
    held = [value]
    for _ in range(3):
        held.append(send(held[-1], pairs))
    return held


def dot(a, b):
    return jnp.dot(a, b, preferred_element_type=jnp.float32)


def gathered(rows, first, second):
    near = ring(rows, first)
    early = ring(near[0], second)
    middle = ring(near[1], second)
    late = ring(jnp.concatenate(near[2:], axis=0), second)
    return [jnp.concatenate([early[s], middle[s], late[s]], axis=0) for s in range(4)]


def per_device(
    layer_inputs,
    out_grads,
    hidden_basis,
    output_basis,
    eigenvalues,
    query_inputs,
    query_grads,
    query_owner,
    example_lengths,
):
    z, y, xh, xl, c = (lax.axis_index(name) for name in AXES)
    way = 1 - 2 * c
    tokens, depth = layer_inputs.shape
    width = hidden_basis.shape[1]
    half = tokens // 2
    units = out_grads.shape[1]
    queries = query_owner.shape[0]

    basis_far = send(hidden_basis, OTHER_XH)
    inverse = (1.0 / (eigenvalues + DAMP)).astype(jnp.bfloat16)
    inverse = jnp.where(c == xh, inverse, send(inverse, EIGEN))

    qtok = query_inputs.shape[1]
    blocks = query_inputs[0].reshape(qtok, 16, 2, width)
    mine = lax.dynamic_index_in_dim(blocks, c, axis=2, keepdims=False)
    mine = jnp.broadcast_to(mine.transpose(1, 0, 2)[:, None], (16, 2, qtok, width))
    slots = lax.all_to_all(
        mine.reshape(32, qtok, width), ("z", "y", "xh"), 0, 0, tiled=True
    )
    owner_inputs = jnp.take(slots, query_owner, axis=0)
    slot_grads = lax.all_gather(query_grads, ("z", "y", "xh"), axis=0, tiled=True)
    owner_grads = jnp.take(slot_grads, query_owner, axis=0)

    grads = dot(out_grads, output_basis).astype(jnp.bfloat16).reshape(4, 2, tokens, -1)
    grads_kept = lax.dynamic_index_in_dim(grads, xh, axis=1, keepdims=False)
    grads_far = send(
        lax.dynamic_index_in_dim(grads, 1 - xh, axis=1, keepdims=False), OTHER_XH
    )
    pair = jnp.where(
        xh == 0,
        jnp.concatenate([grads_kept, grads_far], axis=-1),
        jnp.concatenate([grads_far, grads_kept], axis=-1),
    )
    grads_own = lax.all_gather(
        pair.reshape(4 * tokens, -1), ("z", "y"), axis=1, tiled=True
    )
    grads_own = grads_own.reshape(4, tokens, units)
    grads_own = jnp.concatenate(
        [
            lax.dynamic_index_in_dim(grads_own, (y - way * s) % 4, axis=0)
            for s in range(4)
        ],
        axis=0,
    )
    grads_swap = send(grads_own, OTHER_CORE)
    grads_swap = jnp.stack([grads_swap[n] for n in (0, 3, 2, 1)])
    first = c == z % 2
    grads_rel = jnp.stack(
        [
            jnp.where(first, grads_own, grads_swap),
            jnp.where(first, grads_swap, grads_own),
        ]
    )

    outer = jnp.einsum(
        "qsi,qsj->iqj", owner_grads, owner_inputs, preferred_element_type=jnp.float32
    )
    precond = (outer * inverse.astype(jnp.float32)[:, None, :]).astype(jnp.bfloat16)
    mixed = dot(
        grads_rel.reshape(-1, units), precond.reshape(units, queries * width)
    ).reshape(2, 4, tokens, queries, width)

    near = c == xh
    basis_keep = jnp.where(near, hidden_basis, basis_far)
    basis_send = jnp.where(near, basis_far, hidden_basis)
    parts = (
        gathered(layer_inputs[:half], RING_Z, RING_Y),
        gathered(layer_inputs[half:], RING_Y, RING_Z),
    )
    own = (z // 2 == xl, ((z - way) % 4) // 2 == xl)
    scores = [[None, None], [None, None]]
    for p in range(2):
        for part in range(2):
            chunks = [parts[part][s] for s in (p, p + 2)]
            out = [dot(v, basis_send).astype(jnp.bfloat16) for v in chunks]
            keep = [dot(v, basis_keep).astype(jnp.bfloat16) for v in chunks]
            got = send(
                jnp.stack(out).reshape(2, 4, half, width), OTHER_CORE
            ).astype(jnp.float32)
            keep = jnp.stack(keep).reshape(2, 4, half, width).astype(jnp.float32)
            got = jnp.stack([got[:, n] for n in (0, 3, 2, 1)], axis=1)
            if p == 1:
                got = got[::-1]
            both = (keep + got).astype(jnp.bfloat16)
            if part == 0:
                pairs = [(both[:, n], both[:, n + 2], own[n]) for n in range(2)]
                stay = jnp.stack([jnp.where(o, a, b) for a, b, o in pairs])
                leave = jnp.stack([jnp.where(o, b, a) for a, b, o in pairs])
            else:
                stay = jnp.where(own[p], both[0], both[1])
                leave = jnp.where(own[p], both[1], both[0])
            arrived = send(leave, OTHER_XL)
            hidden = (
                (stay.astype(jnp.float32) + arrived.astype(jnp.float32))
                .astype(jnp.bfloat16)
                .astype(jnp.float32)
            )
            if part == 0:
                block = mixed[:, p::2, :half]
            else:
                block = mixed[p, :, half:]
            scores[part][p] = jnp.sum(block * hidden[..., None, :], axis=-1)
    low = jnp.stack(scores[0], axis=2).reshape(2, 4, half, queries)
    high = jnp.stack(scores[1], axis=0)
    relative = jnp.concatenate([low, high], axis=2).transpose(0, 1, 3, 2)

    z_of = (jnp.arange(2) + z) % 2
    y_of = ((y - jnp.arange(4)) * way) % 4
    placed = jnp.where(first_of(z_of == 0), relative[0][None], relative[1][None])
    pick = y_of[None, :, None] == jnp.arange(4)[None, None, :]
    placed = jnp.sum(
        jnp.where(pick[..., None, None], placed[:, None], 0.0), axis=2
    )
    full = jnp.broadcast_to(
        placed.transpose(1, 0, 2, 3)[:, None, None], (4, 4, 2, 2, queries, tokens)
    )
    meant = (jnp.arange(4) // 2 == xh)[None, :, None, None, None, None]
    full = jnp.where(meant, full, 0.0).reshape(64, queries, tokens)
    terms = lax.all_to_all(full, ("z", "y", "xh", "c"), 0, 0, tiled=True)
    shard_scores = jnp.sum(terms, axis=0)

    index = 2 * (y % 2) + xh
    per_out = tokens // 4
    token_out = lax.dynamic_slice_in_dim(shard_scores, index * per_out, per_out, 1)
    shard = 8 * (2 * xl + c) + 2 * z + y // 2
    lengths = lax.dynamic_index_in_dim(example_lengths, shard, axis=0, keepdims=False)
    at = jnp.arange(lengths.shape[0])
    start = jnp.sum(jnp.where(at < index, lengths, 0))
    end = jnp.sum(jnp.where(at <= index, lengths, 0))
    position = jnp.arange(tokens)
    inside = (position >= start) & (position < end)
    example_out = jnp.sum(jnp.where(inside, shard_scores, 0.0), axis=1, keepdims=True)
    return token_out, example_out


def first_of(flags):
    return flags[:, None, None, None]


def solution(mesh):
    fine = Mesh(mesh.devices.reshape(SIZES), AXES)
    ex, eig = ("z", "y", "xh"), ("xl", "c")
    placed = (
        P(ex, eig),
        P(eig, None),
        P(eig, ex),
        P(None, ex),
        P(None, ex),
        P(ex, None, None),
        P(ex, None, None),
        P(),
        P(),
    )
    out = P(None, eig + ex)
    return jax.shard_map(
        per_device, mesh=fine, in_specs=placed, out_specs=(out, out), check_vma=False
    )
```

```python
import jax
import jax.numpy as jnp
import numpy as np
from jax import lax
from jax.experimental import pallas as pl
from jax.experimental.pallas import tpu as pltpu
from jax.sharding import Mesh, PartitionSpec as P

DAMP = 480
AXES = ("z", "y", "xh", "xl", "c")
SIZES = (4, 4, 2, 2, 2)


def permutation(move):
    pairs = []
    for source, place in enumerate(np.ndindex(*SIZES)):
        target = tuple(a % b for a, b in zip(move(*place), SIZES))
        pairs.append((source, int(np.ravel_multi_index(target, SIZES))))
    return pairs


RING_Z = permutation(lambda z, y, xh, xl, c: (z + 1 - 2 * c, y, xh, xl, c))
RING_Y = permutation(lambda z, y, xh, xl, c: (z, y + 1 - 2 * c, xh, xl, c))
OTHER_XH = permutation(lambda z, y, xh, xl, c: (z, y, xh + 1, xl, c))
OTHER_XL = permutation(lambda z, y, xh, xl, c: (z, y, xh, xl + 1, c))
OTHER_CORE = permutation(lambda z, y, xh, xl, c: (z, y, xh, xl, c + 1))
NEXT_XH = permutation(lambda z, y, xh, xl, c: (z, y, xh + 1, xl + 1, c))


def send(value, pairs):
    return lax.ppermute(value, AXES, pairs)


def after(done, later):
    return lax.optimization_barrier((done, later))


def dot(a, b):
    return jnp.dot(a, b, preferred_element_type=jnp.float32)


def precond_kernel(at, *refs):
    near, far, grads = refs[0:4], refs[4:8], refs[8:12]
    inputs, out = refs[12:]
    x = pl.program_id(0)
    block = grads[0].shape[0]
    for k in range(4):
        inv = jnp.where(x == 0, near[k][...], far[k][...]).astype(jnp.float32).T
        for q in range(out.shape[1]):
            outer = dot(grads[k][...], inputs[0, q])
            out[0, q, k * block : (k + 1) * block, :] = (outer * inv).astype(
                jnp.bfloat16
            )


def precond_of(places, near, far, grads, inputs):
    _, queries, depth, width = inputs.shape
    units = near.shape[1]
    block = units // 16

    def columns(k):
        return pl.BlockSpec((width, block), lambda x, at: (0, at[k]))

    def lines(k):
        return pl.BlockSpec((block, depth), lambda x, at: (at[k], 0))

    def each(*dims):
        return pl.BlockSpec((1, *dims), lambda x, at: (x, 0, 0, 0))

    return pl.pallas_call(
        precond_kernel,
        grid_spec=pltpu.PrefetchScalarGridSpec(
            num_scalar_prefetch=1,
            grid=(2,),
            in_specs=[columns(k) for k in range(4)] * 2
            + [lines(k) for k in range(4)]
            + [each(queries, depth, width)],
            out_specs=each(queries, 4 * block, width),
        ),
        out_shape=jax.ShapeDtypeStruct((2, queries, 4 * block, width), jnp.bfloat16),
        compiler_params=pltpu.CompilerParams(vmem_limit_bytes=40 * 1024 * 1024),
        cost_estimate=pl.CostEstimate(
            flops=2 * 2 * 4 * block * depth * width * queries,
            bytes_accessed=20_000_000,
            transcendentals=0,
        ),
    )(places, *[near] * 4, *[far] * 4, *[grads] * 4, inputs)


def per_device(
    layer_inputs,
    out_grads,
    hidden_basis,
    output_basis,
    eigenvalues,
    query_inputs,
    query_grads,
    query_owner,
    example_lengths,
):
    z, y, xh, xl, c = (lax.axis_index(name) for name in AXES)
    way = 1 - 2 * c
    tokens = layer_inputs.shape[0]
    width = hidden_basis.shape[1]
    units = out_grads.shape[1]
    queries = query_owner.shape[0]
    qtok = query_inputs.shape[1]
    ex, plane = ("z", "y", "xh"), ("z", "y")

    slot = jnp.concatenate([query_inputs[0], query_grads[0]], axis=-1)
    slot_far = send(slot, OTHER_XH)
    grads = dot(out_grads, output_basis).astype(jnp.bfloat16).reshape(4, 2, tokens, -1)
    grads_kept = lax.dynamic_index_in_dim(grads, xh, axis=1, keepdims=False)
    grads_far = send(
        lax.dynamic_index_in_dim(grads, 1 - xh, axis=1, keepdims=False), OTHER_XH
    )
    gathered = lax.all_gather(layer_inputs, plane, axis=0, tiled=True)
    inverse = (1.0 / (eigenvalues.T + DAMP)).astype(jnp.bfloat16)
    (grads_far, slot_far), inverse = after((grads_far, slot_far), inverse)
    part = units // 2
    mine = lax.dynamic_slice_in_dim(inverse, c * part, part, axis=1)
    eigen_half = send(mine, NEXT_XH)

    pair = jnp.where(
        xh == 0,
        jnp.concatenate([grads_kept, grads_far], axis=-1),
        jnp.concatenate([grads_far, grads_kept], axis=-1),
    ).reshape(4 * tokens, -1)
    near_z = [pair, send(pair, RING_Z)]

    slots = jnp.where(
        xh == 0, jnp.stack([slot, slot_far]), jnp.stack([slot_far, slot])
    )
    columns = slots[..., : 16 * 2 * width].reshape(2, qtok, 16, 2 * width)
    of_grads = slots[..., 16 * 2 * width :].reshape(2, qtok, 16, units // 16)
    slots = jnp.concatenate([columns, of_grads], axis=-1).transpose(2, 0, 1, 3)
    slots = lax.all_to_all(slots, plane, 0, 0, tiled=True)
    owned = jnp.take(slots.reshape(32, qtok, -1), query_owner, axis=0)
    owner_grads = lax.all_to_all(
        jnp.broadcast_to(
            owned[None, ..., 2 * width :], (16, queries, qtok, units // 16)
        ),
        plane,
        0,
        0,
        tiled=True,
    )
    near_z[1], owner_grads = lax.optimization_barrier((near_z[1], owner_grads))
    near_z.append(send(near_z[-1], RING_Z))
    owner_grads = owner_grads.transpose(0, 3, 1, 2).reshape(units, queries * qtok)
    owned = owned[..., : 2 * width].reshape(queries, qtok, 2, width)
    owned = owned.transpose(2, 0, 1, 3)
    owned = jnp.where(xh == 0, owned, owned[::-1])
    owner_inputs = jnp.where(
        jnp.eye(queries, dtype=jnp.bool_)[:, :, None, None], owned[:, None], 0
    ).reshape(2, queries, queries * qtok, width)

    basis = jnp.split(hidden_basis, (1024, 2304), axis=0)
    (near_z[2], eigen_half), basis = after((near_z[2], eigen_half), basis)
    basis_far = [send(v, OTHER_XH) for v in basis[:2]]
    near_z.append(send(near_z[-1], RING_Z))
    steps = [jnp.stack(near_z)]
    steps.append(send(steps[0], RING_Y))
    eigen_other = send(eigen_half, OTHER_CORE)
    inverse_far = jnp.where(
        c == 0,
        jnp.concatenate([eigen_half, eigen_other], axis=1),
        jnp.concatenate([eigen_other, eigen_half], axis=1),
    )
    preconds = []
    for s in range(4):
        places = (z - way * jnp.arange(4)) % 4 * 4 + (y - way * s) % 4
        preconds.append(
            precond_of(
                places.astype(jnp.int32),
                inverse,
                inverse_far,
                owner_grads,
                owner_inputs,
            )
        )

    def mix(s):
        rows = steps[s].transpose(1, 0, 2).reshape(4 * tokens, units // 4)
        return jnp.einsum(
            "ti,xqij->xqtj", rows, preconds[s], preferred_element_type=jnp.float32
        ).astype(jnp.bfloat16)

    (basis_far, preconds, steps[1]), basis[2] = after(
        (basis_far, preconds, steps[1]), basis[2]
    )
    basis_far.append(send(basis[2], OTHER_XH))
    steps.append(send(steps[1], RING_Y))
    steps.append(send(steps[2], RING_Y))
    early = sum(mix(s).astype(jnp.float32) for s in range(3)).astype(jnp.bfloat16)
    late = mix(3)

    basis_far = jnp.concatenate(basis_far, axis=0)
    blocks = gathered.reshape(4, 4 * tokens, -1)

    def products(z_block, basis):
        rows = lax.dynamic_index_in_dim(blocks, z_block, axis=0, keepdims=False)
        return dot(rows, basis).astype(jnp.bfloat16)

    def total(one, two):
        return (one.astype(jnp.float32) + two.astype(jnp.float32)).astype(jnp.bfloat16)

    sides = (hidden_basis, basis_far)
    there = [products(2 * (1 - xl) + 1 - c, b) for b in sides]
    there = [send(v, OTHER_CORE) for v in there]
    leave = [products(2 * (1 - xl) + c, b) for b in sides]
    leave = [total(a, b) for a, b in zip(leave, there)]
    arrived = [send(v, OTHER_XL) for v in leave]
    there = [products(2 * xl + 1 - c, b) for b in sides]
    there = [send(v, OTHER_CORE) for v in there]
    stay = [products(2 * xl + c, b) for b in sides]
    stay = [total(a, b) for a, b in zip(stay, there)]
    hidden = jnp.stack([total(a, b) for a, b in zip(stay, arrived)])
    mixed = early.astype(jnp.float32) + late.astype(jnp.float32)
    scores = jnp.sum(mixed * hidden.astype(jnp.float32)[:, None], axis=(0, 3))
    scores = scores.reshape(queries, 4, tokens)

    full = jnp.broadcast_to(
        scores.transpose(1, 0, 2)[:, None, None], (4, 4, 2, queries, tokens)
    )
    meant = (jnp.arange(4) // 2 == xh)[None, :, None, None, None]
    full = jnp.where(meant, full, 0.0).reshape(32, queries, tokens)
    terms = lax.all_to_all(full, ex, 0, 0, tiled=True)
    shard_scores = jnp.sum(terms, axis=0)

    index = 2 * (y % 2) + xh
    per_out = tokens // 4
    token_out = lax.dynamic_slice_in_dim(shard_scores, index * per_out, per_out, 1)
    shard = 8 * (2 * xl + c) + 2 * z + y // 2
    lengths = lax.dynamic_index_in_dim(example_lengths, shard, axis=0, keepdims=False)
    at = jnp.arange(lengths.shape[0])
    start = jnp.sum(jnp.where(at < index, lengths, 0))
    end = jnp.sum(jnp.where(at <= index, lengths, 0))
    position = jnp.arange(tokens)
    inside = (position >= start) & (position < end)
    example_out = jnp.sum(jnp.where(inside, shard_scores, 0.0), axis=1, keepdims=True)
    return token_out, example_out


def solution(mesh):
    fine = Mesh(mesh.devices.reshape(SIZES), AXES)
    ex, eig = ("z", "y", "xh"), ("xl", "c")
    placed = (
        P(ex, eig),
        P(eig, None),
        P(eig, ex),
        P(None, ex),
        P(None, ex),
        P(ex, None, None),
        P(ex, None, None),
        P(),
        P(),
    )
    out = P(None, eig + ex)
    return jax.shard_map(
        per_device, mesh=fine, in_specs=placed, out_specs=(out, out), check_vma=False
    )
```

```python
import functools

import jax
import jax.numpy as jnp
import numpy as np
from jax import lax
from jax.experimental import pallas as pl
from jax.experimental.pallas import tpu as pltpu
from jax.sharding import Mesh, PartitionSpec as P

DAMP = 480
AXES = ("z", "y", "xh", "xl", "c")
SIZES = (4, 4, 2, 2, 2)


def permutation(move):
    pairs = []
    for source, place in enumerate(np.ndindex(*SIZES)):
        target = tuple(a % b for a, b in zip(move(*place), SIZES))
        pairs.append((source, int(np.ravel_multi_index(target, SIZES))))
    return pairs


RING_Z = permutation(lambda z, y, xh, xl, c: (z + 1 - 2 * c, y, xh, xl, c))
RING_Y = permutation(lambda z, y, xh, xl, c: (z, y + 1 - 2 * c, xh, xl, c))
OTHER_XH = permutation(lambda z, y, xh, xl, c: (z, y, xh + 1, xl, c))
OTHER_XL = permutation(lambda z, y, xh, xl, c: (z, y, xh, xl + 1, c))
OTHER_CORE = permutation(lambda z, y, xh, xl, c: (z, y, xh, xl, c + 1))
NEXT_XH = permutation(lambda z, y, xh, xl, c: (z, y, xh + 1, xl + 1, c))


def send(value, pairs):
    return lax.ppermute(value, AXES, pairs)


def after(done, later):
    return lax.optimization_barrier((done, later))


def dot(a, b):
    return jnp.dot(a, b, preferred_element_type=jnp.float32)


def precond_kernel(at, *refs):
    near, far, grads = refs[0:4], refs[4:8], refs[8:12]
    inputs, out = refs[12:]
    x = pl.program_id(1)
    block = grads[0].shape[0]
    for k in range(4):
        inv = jnp.where(x == 0, near[k][...], far[k][...]).astype(jnp.float32).T
        for q in range(out.shape[1]):
            outer = dot(grads[k][...], inputs[0, q])
            out[0, q, k * block : (k + 1) * block, :] = (outer * inv).astype(
                jnp.bfloat16
            )


def precond_of(places, near, far, grads, inputs):
    _, queries, depth, width = inputs.shape
    units = near.shape[1]
    block = units // 16
    blocks = places.shape[0] // 2

    def columns(k):
        return pl.BlockSpec((width, block), lambda s, x, at: (0, at[4 * s + k]))

    def lines(k):
        return pl.BlockSpec((block, depth), lambda s, x, at: (at[4 * s + k], 0))

    return pl.pallas_call(
        precond_kernel,
        grid_spec=pltpu.PrefetchScalarGridSpec(
            num_scalar_prefetch=1,
            grid=(blocks // 4, 2),
            in_specs=[columns(k) for k in range(4)]
            + [columns(blocks + k) for k in range(4)]
            + [lines(k) for k in range(4)]
            + [
                pl.BlockSpec(
                    (1, queries, depth, width), lambda s, x, at: (x, 0, 0, 0)
                )
            ],
            out_specs=pl.BlockSpec(
                (1, queries, 4 * block, width),
                lambda s, x, at: (x, 0, s, 0),
            ),
        ),
        out_shape=jax.ShapeDtypeStruct(
            (2, queries, blocks * block, width), jnp.bfloat16
        ),
        compiler_params=pltpu.CompilerParams(vmem_limit_bytes=18 * 1024 * 1024),
        cost_estimate=pl.CostEstimate(
            flops=2 * 2 * blocks * block * depth * width * queries,
            bytes_accessed=5_000_000 * blocks,
            transcendentals=0,
        ),
    )(places, *[near] * 4, *[far] * 4, *[grads] * 4, inputs)


def mixed_kernel(chunks, *refs):
    steps, preconds, before = refs[:chunks], refs[chunks : 2 * chunks], refs[2 * chunks : -2]
    out, wide = refs[-2:]
    block = steps[0].shape[-1]

    @pl.when((pl.program_id(0) == 0) & (pl.program_id(1) == 0))
    def _():
        for s in range(chunks):
            for n in range(4):
                wide[s, :, n * block : (n + 1) * block] = steps[s][n]

    total = before[0][0, 0].astype(jnp.float32) if before else 0.0
    for s in range(chunks):
        total += dot(wide[s], preconds[s][0, 0])
    out[0, 0] = total.astype(jnp.bfloat16)


def mixed_of(steps, precond, start, *before):
    _, queries, units, width = precond.shape
    _, tokens, block = steps[0].shape
    chunks = len(steps)
    each = pl.BlockSpec((1, 1, tokens, width), lambda x, q: (x, q, 0, 0))

    def chunk(s):
        return pl.BlockSpec((1, 1, units // 4, width), lambda x, q: (x, q, s, 0))

    return pl.pallas_call(
        functools.partial(mixed_kernel, chunks),
        grid=(2, queries),
        in_specs=[
            pl.BlockSpec(
                (4, tokens, block), lambda x, q: (0, 0, 0), pipeline_mode=pl.Buffered(1)
            )
        ]
        * chunks
        + [chunk(start + s) for s in range(chunks)]
        + [each] * len(before),
        out_specs=each,
        out_shape=jax.ShapeDtypeStruct((2, queries, tokens, width), jnp.bfloat16),
        scratch_shapes=[pltpu.VMEM((chunks, tokens, units // 4), jnp.bfloat16)],
        compiler_params=pltpu.CompilerParams(vmem_limit_bytes=24 * 1024 * 1024),
        cost_estimate=pl.CostEstimate(
            flops=chunks * queries * tokens * units * width,
            bytes_accessed=10_000_000 * chunks,
            transcendentals=0,
        ),
    )(*steps, *[precond] * chunks, *before)


def products_kernel(at, rows, basis, out):
    made = lax.dot_general(
        rows[...],
        basis[...],
        (((1,), (1,)), ((), ())),
        preferred_element_type=jnp.float32,
    )
    out[0] = made.astype(jnp.bfloat16)


def products_of(z_blocks, gathered, basis):
    groups = z_blocks.shape[0]
    width, depth = basis.shape
    tokens = gathered.shape[0] // 4
    part = tokens // 2
    out = pl.pallas_call(
        products_kernel,
        grid_spec=pltpu.PrefetchScalarGridSpec(
            num_scalar_prefetch=1,
            grid=(groups, 2),
            in_specs=[
                pl.BlockSpec((part, depth), lambda g, r, at: (2 * at[g] + r, 0)),
                pl.BlockSpec(
                    (width, depth), lambda g, r, at: (0, 0), pipeline_mode=pl.Buffered(1)
                ),
            ],
            out_specs=pl.BlockSpec((1, part, width), lambda g, r, at: (g, r, 0)),
        ),
        out_shape=jax.ShapeDtypeStruct((groups, tokens, width), jnp.bfloat16),
        compiler_params=pltpu.CompilerParams(vmem_limit_bytes=52 * 1024 * 1024),
        cost_estimate=pl.CostEstimate(
            flops=2 * groups * tokens * depth * width,
            bytes_accessed=4_000_000 * groups,
            transcendentals=0,
        ),
    )(z_blocks, gathered, basis)
    return [out[g] for g in range(groups)]


def score_kernel(mixed, stay, stay_far, arrived, arrived_far, out):
    hidden = []
    for a, b in ((stay, arrived), (stay_far, arrived_far)):
        both = a[...].astype(jnp.float32) + b[...].astype(jnp.float32)
        hidden.append(both.astype(jnp.bfloat16).astype(jnp.float32))
    for q in range(out.shape[0]):
        terms = sum(mixed[x, q].astype(jnp.float32) * hidden[x] for x in range(2))
        out[q, :] = jnp.sum(terms, axis=-1)


def scores_of(mixed, stay, arrived):
    _, queries, tokens, width = mixed.shape
    rows = 128
    part = pl.BlockSpec((rows, width), lambda t: (t, 0))
    return pl.pallas_call(
        score_kernel,
        grid=(tokens // rows,),
        in_specs=[pl.BlockSpec((2, queries, rows, width), lambda t: (0, 0, t, 0))]
        + [part] * 4,
        out_specs=pl.BlockSpec((queries, rows), lambda t: (0, t)),
        out_shape=jax.ShapeDtypeStruct((queries, tokens), jnp.float32),
        compiler_params=pltpu.CompilerParams(vmem_limit_bytes=16 * 1024 * 1024),
        cost_estimate=pl.CostEstimate(
            flops=4 * queries * tokens * width,
            bytes_accessed=6_000_000,
            transcendentals=0,
        ),
    )(mixed, *stay, *arrived)


def per_device(
    layer_inputs,
    out_grads,
    hidden_basis,
    output_basis,
    eigenvalues,
    query_inputs,
    query_grads,
    query_owner,
    example_lengths,
):
    z, y, xh, xl, c = (lax.axis_index(name) for name in AXES)
    way = 1 - 2 * c
    tokens = layer_inputs.shape[0]
    width = hidden_basis.shape[1]
    units = out_grads.shape[1]
    queries = query_owner.shape[0]
    qtok = query_inputs.shape[1]
    ex, plane = ("z", "y", "xh"), ("z", "y")

    slot = jnp.concatenate([query_inputs[0], query_grads[0]], axis=-1)
    slot_far = send(slot, OTHER_XH)
    grads = dot(out_grads, output_basis).astype(jnp.bfloat16).reshape(4, 2, tokens, -1)
    grads_kept = lax.dynamic_index_in_dim(grads, xh, axis=1, keepdims=False)
    grads_far = send(
        lax.dynamic_index_in_dim(grads, 1 - xh, axis=1, keepdims=False), OTHER_XH
    )
    gathered = lax.all_gather(layer_inputs, plane, axis=0, tiled=True)
    inverse = (1.0 / (eigenvalues.T + DAMP)).astype(jnp.bfloat16)
    grads_far, inverse = after(grads_far, inverse)
    part = units // 2
    mine = lax.dynamic_slice_in_dim(inverse, c * part, part, axis=1)
    eigen_half = send(mine, NEXT_XH)

    pair = jnp.where(
        xh == 0,
        jnp.concatenate([grads_kept, grads_far], axis=-1),
        jnp.concatenate([grads_far, grads_kept], axis=-1),
    ).reshape(4 * tokens, -1)
    near_z = [pair, send(pair, RING_Z)]
    near_z[1], (slot, slot_far) = after(near_z[1], (slot, slot_far))
    near_z.append(send(near_z[-1], RING_Z))
    near_z.append(send(near_z[-1], RING_Z))

    slots = jnp.where(
        xh == 0, jnp.stack([slot, slot_far]), jnp.stack([slot_far, slot])
    )
    columns = slots[..., : 16 * 2 * width].reshape(2, qtok, 16, 2 * width)
    of_grads = slots[..., 16 * 2 * width :].reshape(2, qtok, 16, units // 16)
    slots = jnp.concatenate([columns, of_grads], axis=-1).transpose(2, 0, 1, 3)
    slots = lax.all_to_all(slots, plane, 0, 0, tiled=True)
    (slots, eigen_half, near_z[2]), basis = after(
        (slots, eigen_half, near_z[2]), hidden_basis
    )
    owned = jnp.take(slots.reshape(32, qtok, -1), query_owner, axis=0)
    owner_grads = lax.all_to_all(
        jnp.broadcast_to(
            owned[None, ..., 2 * width :], (16, queries, qtok, units // 16)
        ),
        plane,
        0,
        0,
        tiled=True,
    )
    owner_grads = owner_grads.transpose(0, 3, 1, 2).reshape(units, queries * qtok)
    owned = owned[..., : 2 * width].reshape(queries, qtok, 2, width)
    owned = owned.transpose(2, 0, 1, 3)
    owned = jnp.where(xh == 0, owned, owned[::-1])
    owner_inputs = jnp.where(
        jnp.eye(queries, dtype=jnp.bool_)[:, :, None, None], owned[:, None], 0
    ).reshape(2, queries, queries * qtok, width)

    basis_far = send(basis, OTHER_XH)
    near_z[3], owner_grads = lax.optimization_barrier((near_z[3], owner_grads))
    steps = [jnp.stack(near_z)]
    steps.append(send(steps[0], RING_Y))
    eigen_other = send(eigen_half, OTHER_CORE)
    inverse_far = jnp.concatenate([eigen_half, eigen_other], axis=1)

    def precond(chunks):
        places = [
            (z - way * jnp.arange(4)) % 4 * 4 + (y - way * s) % 4 for s in chunks
        ]
        places = jnp.concatenate(places).astype(jnp.int32)
        return precond_of(
            jnp.concatenate([places, (places + 8 * c) % 16]),
            inverse,
            inverse_far,
            owner_grads,
            owner_inputs,
        )

    preconds = precond((0, 1, 2, 3))
    early = mixed_of(steps[:1], preconds, 0)
    early, preconds, steps[1] = lax.optimization_barrier((early, preconds, steps[1]))
    steps.append(send(steps[1], RING_Y))


    def swapped(values, pairs):
        return [send(v, pairs) for v in values]

    def total(one, two):
        return [
            (a.astype(jnp.float32) + b.astype(jnp.float32)).astype(jnp.bfloat16)
            for a, b in zip(one, two)
        ]

    z_blocks = 2 * jnp.stack([1 - xl, 1 - xl, xl, xl]) + jnp.stack([1 - c, c] * 2)
    z_blocks = z_blocks.astype(jnp.int32)
    made = products_of(z_blocks, gathered, hidden_basis.T)
    made, basis_far, steps[2] = lax.optimization_barrier((made, basis_far, steps[2]))
    steps.append(send(steps[2], RING_Y))
    made_far = products_of(z_blocks[:2], gathered, basis_far.T)
    made_far, steps[3], gathered = lax.optimization_barrier(
        (made_far, steps[3], gathered)
    )
    made_far += products_of(z_blocks[2:], gathered, basis_far.T)
    there, here, there_last, here_last = zip(made, made_far)
    leave = total(here, swapped(there, OTHER_CORE))
    arrived = swapped(leave, OTHER_XL)
    stay = total(here_last, swapped(there_last, OTHER_CORE))
    steps[3], early, leave, stay = lax.optimization_barrier(
        (steps[3], early, leave, stay)
    )
    mixed = mixed_of(steps[1:], preconds, 1, early)
    mixed, arrived = lax.optimization_barrier((mixed, arrived))
    scores = scores_of(mixed, stay, arrived)
    scores = scores.reshape(queries, 4, tokens)

    full = jnp.broadcast_to(
        scores.transpose(1, 0, 2)[:, None, None], (4, 4, 2, queries, tokens)
    )
    meant = (jnp.arange(4) // 2 == xh)[None, :, None, None, None]
    full = jnp.where(meant, full, 0.0).reshape(32, queries, tokens)
    terms = lax.all_to_all(full, ex, 0, 0, tiled=True)
    shard_scores = jnp.sum(terms, axis=0)

    index = 2 * (y % 2) + xh
    per_out = tokens // 4
    token_out = lax.dynamic_slice_in_dim(shard_scores, index * per_out, per_out, 1)
    shard = 8 * (2 * xl + c) + 2 * z + y // 2
    lengths = lax.dynamic_index_in_dim(example_lengths, shard, axis=0, keepdims=False)
    at = jnp.arange(lengths.shape[0])
    start = jnp.sum(jnp.where(at < index, lengths, 0))
    end = jnp.sum(jnp.where(at <= index, lengths, 0))
    position = jnp.arange(tokens)
    inside = (position >= start) & (position < end)
    example_out = jnp.sum(jnp.where(inside, shard_scores, 0.0), axis=1, keepdims=True)
    return token_out, example_out


def solution(mesh):
    fine = Mesh(mesh.devices.reshape(SIZES), AXES)
    ex, eig = ("z", "y", "xh"), ("xl", "c")
    placed = (
        P(ex, eig),
        P(eig, None),
        P(eig, ex),
        P(None, ex),
        P(None, ex),
        P(ex, None, None),
        P(ex, None, None),
        P(),
        P(),
    )
    out = P(None, eig + ex)
    return jax.shard_map(
        per_device, mesh=fine, in_specs=placed, out_specs=(out, out), check_vma=False
    )
```

```python
import functools

import jax
import jax.numpy as jnp
import numpy as np
from jax import lax
from jax.experimental import pallas as pl
from jax.experimental.pallas import tpu as pltpu
from jax.sharding import Mesh, PartitionSpec as P

DAMP = 480
AXES = ("z", "y", "xh", "xl", "c")
SIZES = (4, 4, 2, 2, 2)


def permutation(move):
    pairs = []
    for source, place in enumerate(np.ndindex(*SIZES)):
        target = tuple(a % b for a, b in zip(move(*place), SIZES))
        pairs.append((source, int(np.ravel_multi_index(target, SIZES))))
    return pairs


RING_Z = permutation(lambda z, y, xh, xl, c: (z + 1 - 2 * c, y, xh, xl, c))
RING_Y = permutation(lambda z, y, xh, xl, c: (z, y + 1 - 2 * c, xh, xl, c))
OTHER_XH = permutation(lambda z, y, xh, xl, c: (z, y, xh + 1, xl, c))
OTHER_XL = permutation(lambda z, y, xh, xl, c: (z, y, xh, xl + 1, c))
OTHER_CORE = permutation(lambda z, y, xh, xl, c: (z, y, xh, xl, c + 1))
NEXT_XH = permutation(lambda z, y, xh, xl, c: (z, y, xh + 1, xl + 1, c))


def send(value, pairs):
    return lax.ppermute(value, AXES, pairs)


def after(done, later):
    return lax.optimization_barrier((done, later))


def dot(a, b):
    return jnp.dot(a, b, preferred_element_type=jnp.float32)


def precond_kernel(at, *refs):
    near, far, grads = refs[0:4], refs[4:8], refs[8:12]
    inputs, out = refs[12:]
    x = pl.program_id(1)
    block = grads[0].shape[0]
    for k in range(4):
        inv = jnp.where(x == 0, near[k][...], far[k][...]).astype(jnp.float32).T
        for q in range(out.shape[1]):
            outer = dot(grads[k][...], inputs[0, q])
            out[0, q, k * block : (k + 1) * block, :] = (outer * inv).astype(
                jnp.bfloat16
            )


def precond_of(places, near, far, grads, inputs):
    _, queries, depth, width = inputs.shape
    units = near.shape[1]
    block = units // 16
    blocks = places.shape[0] // 2

    def columns(k):
        return pl.BlockSpec((width, block), lambda s, x, at: (0, at[4 * s + k]))

    def lines(k):
        return pl.BlockSpec((block, depth), lambda s, x, at: (at[4 * s + k], 0))

    return pl.pallas_call(
        precond_kernel,
        grid_spec=pltpu.PrefetchScalarGridSpec(
            num_scalar_prefetch=1,
            grid=(blocks // 4, 2),
            in_specs=[columns(k) for k in range(4)]
            + [columns(blocks + k) for k in range(4)]
            + [lines(k) for k in range(4)]
            + [
                pl.BlockSpec(
                    (1, queries, depth, width), lambda s, x, at: (x, 0, 0, 0)
                )
            ],
            out_specs=pl.BlockSpec(
                (1, queries, 4 * block, width),
                lambda s, x, at: (x, 0, s, 0),
            ),
        ),
        out_shape=jax.ShapeDtypeStruct(
            (2, queries, blocks * block, width), jnp.bfloat16
        ),
        compiler_params=pltpu.CompilerParams(vmem_limit_bytes=18 * 1024 * 1024),
        cost_estimate=pl.CostEstimate(
            flops=2 * 2 * blocks * block * depth * width * queries,
            bytes_accessed=5_000_000 * blocks,
            transcendentals=0,
        ),
    )(places, *[near] * 4, *[far] * 4, *[grads] * 4, inputs)


def mixed_kernel(chunks, *refs):
    steps, preconds, before = refs[:chunks], refs[chunks : 2 * chunks], refs[2 * chunks : -2]
    out, wide = refs[-2:]
    block = steps[0].shape[-1]

    @pl.when((pl.program_id(0) == 0) & (pl.program_id(1) == 0))
    def _():
        for s in range(chunks):
            for n in range(4):
                wide[s, :, n * block : (n + 1) * block] = steps[s][n]

    total = before[0][0, 0].astype(jnp.float32) if before else 0.0
    for s in range(chunks):
        total += dot(wide[s], preconds[s][0, 0])
    out[0, 0] = total.astype(jnp.bfloat16)


def mixed_of(steps, precond, start, *before):
    _, queries, units, width = precond.shape
    _, tokens, block = steps[0].shape
    chunks = len(steps)
    each = pl.BlockSpec((1, 1, tokens, width), lambda x, q: (x, q, 0, 0))

    def chunk(s):
        return pl.BlockSpec((1, 1, units // 4, width), lambda x, q: (x, q, s, 0))

    return pl.pallas_call(
        functools.partial(mixed_kernel, chunks),
        grid=(2, queries),
        in_specs=[
            pl.BlockSpec(
                (4, tokens, block), lambda x, q: (0, 0, 0), pipeline_mode=pl.Buffered(1)
            )
        ]
        * chunks
        + [chunk(start + s) for s in range(chunks)]
        + [each] * len(before),
        out_specs=each,
        out_shape=jax.ShapeDtypeStruct((2, queries, tokens, width), jnp.bfloat16),
        scratch_shapes=[pltpu.VMEM((chunks, tokens, units // 4), jnp.bfloat16)],
        compiler_params=pltpu.CompilerParams(vmem_limit_bytes=24 * 1024 * 1024),
        cost_estimate=pl.CostEstimate(
            flops=chunks * queries * tokens * units * width,
            bytes_accessed=10_000_000 * chunks,
            transcendentals=0,
        ),
    )(*steps, *[precond] * chunks, *before)


def products_kernel(at, rows, basis, out):
    made = lax.dot_general(
        rows[...],
        basis[...],
        (((1,), (1,)), ((), ())),
        preferred_element_type=jnp.float32,
    )
    out[0] = made.astype(jnp.bfloat16)


def products_of(z_blocks, gathered, basis):
    groups = z_blocks.shape[0]
    width, depth = basis.shape
    tokens = gathered.shape[0] // 4
    part = tokens // 2
    out = pl.pallas_call(
        products_kernel,
        grid_spec=pltpu.PrefetchScalarGridSpec(
            num_scalar_prefetch=1,
            grid=(groups, 2),
            in_specs=[
                pl.BlockSpec((part, depth), lambda g, r, at: (2 * at[g] + r, 0)),
                pl.BlockSpec(
                    (width, depth), lambda g, r, at: (0, 0), pipeline_mode=pl.Buffered(1)
                ),
            ],
            out_specs=pl.BlockSpec((1, part, width), lambda g, r, at: (g, r, 0)),
        ),
        out_shape=jax.ShapeDtypeStruct((groups, tokens, width), jnp.bfloat16),
        compiler_params=pltpu.CompilerParams(vmem_limit_bytes=52 * 1024 * 1024),
        cost_estimate=pl.CostEstimate(
            flops=2 * groups * tokens * depth * width,
            bytes_accessed=4_000_000 * groups,
            transcendentals=0,
        ),
    )(z_blocks, gathered, basis)
    return out


def score_kernel(mixed, stay, stay_far, arrived, arrived_far, out):
    hidden = []
    for a, b in ((stay, arrived), (stay_far, arrived_far)):
        both = a[...].astype(jnp.float32) + b[...].astype(jnp.float32)
        hidden.append(both.astype(jnp.bfloat16).astype(jnp.float32))
    for q in range(out.shape[0]):
        terms = sum(mixed[x, q].astype(jnp.float32) * hidden[x] for x in range(2))
        out[q, :] = jnp.sum(terms, axis=-1)


def scores_of(mixed, stay, arrived):
    _, queries, tokens, width = mixed.shape
    rows = 128
    part = pl.BlockSpec((rows, width), lambda t: (t, 0))
    return pl.pallas_call(
        score_kernel,
        grid=(tokens // rows,),
        in_specs=[pl.BlockSpec((2, queries, rows, width), lambda t: (0, 0, t, 0))]
        + [part] * 4,
        out_specs=pl.BlockSpec((queries, rows), lambda t: (0, t)),
        out_shape=jax.ShapeDtypeStruct((queries, tokens), jnp.float32),
        compiler_params=pltpu.CompilerParams(vmem_limit_bytes=16 * 1024 * 1024),
        cost_estimate=pl.CostEstimate(
            flops=4 * queries * tokens * width,
            bytes_accessed=6_000_000,
            transcendentals=0,
        ),
    )(mixed, *stay, *arrived)


def per_device(
    layer_inputs,
    out_grads,
    hidden_basis,
    output_basis,
    eigenvalues,
    query_inputs,
    query_grads,
    query_owner,
    example_lengths,
):
    z, y, xh, xl, c = (lax.axis_index(name) for name in AXES)
    way = 1 - 2 * c
    tokens = layer_inputs.shape[0]
    width = hidden_basis.shape[1]
    units = out_grads.shape[1]
    queries = query_owner.shape[0]
    qtok = query_inputs.shape[1]
    ex, plane = ("z", "y", "xh"), ("z", "y")

    slot = jnp.concatenate([query_inputs[0], query_grads[0]], axis=-1)
    slot_far = send(slot, OTHER_XH)
    grads = dot(out_grads, output_basis).astype(jnp.bfloat16).reshape(4, 2, tokens, -1)
    grads_kept = lax.dynamic_index_in_dim(grads, xh, axis=1, keepdims=False)
    grads_far = send(
        lax.dynamic_index_in_dim(grads, 1 - xh, axis=1, keepdims=False), OTHER_XH
    )
    gathered = lax.all_gather(layer_inputs, plane, axis=0, tiled=True)
    inverse = (1.0 / (eigenvalues.T + DAMP)).astype(jnp.bfloat16)
    grads_far, inverse = after(grads_far, inverse)
    part = units // 2
    mine = lax.dynamic_slice_in_dim(inverse, c * part, part, axis=1)
    eigen_half = send(mine, NEXT_XH)

    pair = jnp.where(
        xh == 0,
        jnp.concatenate([grads_kept, grads_far], axis=-1),
        jnp.concatenate([grads_far, grads_kept], axis=-1),
    ).reshape(4 * tokens, -1)
    near_z = [pair, send(pair, RING_Z)]
    near_z[1], (slot, slot_far) = after(near_z[1], (slot, slot_far))
    near_z.append(send(near_z[-1], RING_Z))
    near_z.append(send(near_z[-1], RING_Z))

    slots = jnp.where(
        xh == 0, jnp.stack([slot, slot_far]), jnp.stack([slot_far, slot])
    )
    columns = slots[..., : 16 * 2 * width].reshape(2, qtok, 16, 2 * width)
    of_grads = slots[..., 16 * 2 * width :].reshape(2, qtok, 16, units // 16)
    slots = jnp.concatenate([columns, of_grads], axis=-1).transpose(2, 0, 1, 3)
    slots = lax.all_to_all(slots, plane, 0, 0, tiled=True)
    (slots, eigen_half, near_z[2]), basis = after(
        (slots, eigen_half, near_z[2]), hidden_basis
    )
    owned = jnp.take(slots.reshape(32, qtok, -1), query_owner, axis=0)
    owner_grads = lax.all_to_all(
        jnp.broadcast_to(
            owned[None, ..., 2 * width :], (16, queries, qtok, units // 16)
        ),
        plane,
        0,
        0,
        tiled=True,
    )
    owner_grads = owner_grads.transpose(0, 3, 1, 2).reshape(units, queries * qtok)
    owned = owned[..., : 2 * width].reshape(queries, qtok, 2, width)
    owned = owned.transpose(2, 0, 1, 3)
    owned = jnp.where(xh == 0, owned, owned[::-1])
    owner_inputs = jnp.where(
        jnp.eye(queries, dtype=jnp.bool_)[:, :, None, None], owned[:, None], 0
    ).reshape(2, queries, queries * qtok, width)

    basis_far = send(basis, OTHER_XH)
    near_z[3], owner_grads = lax.optimization_barrier((near_z[3], owner_grads))
    steps = [jnp.stack(near_z)]
    steps.append(send(steps[0], RING_Y))
    eigen_other = send(eigen_half, OTHER_CORE)
    inverse_far = jnp.concatenate([eigen_half, eigen_other], axis=1)

    def precond(chunks):
        places = [
            (z - way * jnp.arange(4)) % 4 * 4 + (y - way * s) % 4 for s in chunks
        ]
        places = jnp.concatenate(places).astype(jnp.int32)
        return precond_of(
            jnp.concatenate([places, (places + 8 * c) % 16]),
            inverse,
            inverse_far,
            owner_grads,
            owner_inputs,
        )

    preconds = precond((0, 1, 2, 3))
    early = mixed_of(steps[:1], preconds, 0)
    early, preconds, steps[1] = lax.optimization_barrier((early, preconds, steps[1]))
    steps.append(send(steps[1], RING_Y))


    def swapped(values, pairs):
        return [send(v, pairs) for v in values]

    def total(one, two):
        return [
            (a.astype(jnp.float32) + b.astype(jnp.float32)).astype(jnp.bfloat16)
            for a, b in zip(one, two)
        ]

    z_blocks = 2 * jnp.stack([1 - xl, xl] * 2) + jnp.stack([1 - c, 1 - c, c, c])
    z_blocks = z_blocks.astype(jnp.int32)
    made = products_of(z_blocks, gathered, hidden_basis.T)
    made, basis_far, steps[2] = lax.optimization_barrier((made, basis_far, steps[2]))
    steps.append(send(steps[2], RING_Y))
    far = products_of(z_blocks[:2], gathered, basis_far.T)
    far, steps[3], gathered = lax.optimization_barrier((far, steps[3], gathered))
    here = [made[2:], products_of(z_blocks[2:], gathered, basis_far.T)]
    both = total(here, swapped([made[:2], far], OTHER_CORE))
    leave, stay = ([v[g] for v in both] for g in range(2))
    arrived = swapped(leave, OTHER_XL)
    steps[3], early, leave, stay = lax.optimization_barrier(
        (steps[3], early, leave, stay)
    )
    mixed = mixed_of(steps[1:], preconds, 1, early)
    mixed, arrived = lax.optimization_barrier((mixed, arrived))
    scores = scores_of(mixed, stay, arrived)
    scores = scores.reshape(queries, 4, tokens)

    full = jnp.broadcast_to(
        scores.transpose(1, 0, 2)[:, None, None], (4, 4, 2, queries, tokens)
    )
    meant = (jnp.arange(4) // 2 == xh)[None, :, None, None, None]
    full = jnp.where(meant, full, 0.0).reshape(32, queries, tokens)
    terms = lax.all_to_all(full, ex, 0, 0, tiled=True)
    shard_scores = jnp.sum(terms, axis=0)

    index = 2 * (y % 2) + xh
    per_out = tokens // 4
    token_out = lax.dynamic_slice_in_dim(shard_scores, index * per_out, per_out, 1)
    shard = 8 * (2 * xl + c) + 2 * z + y // 2
    lengths = lax.dynamic_index_in_dim(example_lengths, shard, axis=0, keepdims=False)
    at = jnp.arange(lengths.shape[0])
    start = jnp.sum(jnp.where(at < index, lengths, 0))
    end = jnp.sum(jnp.where(at <= index, lengths, 0))
    position = jnp.arange(tokens)
    inside = (position >= start) & (position < end)
    example_out = jnp.sum(jnp.where(inside, shard_scores, 0.0), axis=1, keepdims=True)
    return token_out, example_out


def solution(mesh):
    fine = Mesh(mesh.devices.reshape(SIZES), AXES)
    ex, eig = ("z", "y", "xh"), ("xl", "c")
    placed = (
        P(ex, eig),
        P(eig, None),
        P(eig, ex),
        P(None, ex),
        P(None, ex),
        P(ex, None, None),
        P(ex, None, None),
        P(),
        P(),
    )
    out = P(None, eig + ex)
    return jax.shard_map(
        per_device, mesh=fine, in_specs=placed, out_specs=(out, out), check_vma=False
    )
```
